32 devices in a mesh: band: 4 (over y, x), fft: 8 (over z, core).
Axes of the slice: x: 2, y: 2, z: 4, core: 2. Of those that a mesh axis runs over, the one named last changes fastest.
Arguments:
- orbitals: float32 [2, 4, 144, 2048], P(None, 'band', None, 'fft'), may hold values from -27 to 27
- potential: float32 [288, 20736], P('fft'), may hold values from -3 to 1
- projectors: float32 [2, 16, 144, 2048], P(None, None, None, 'fft'), may hold values from -6 to 6
- coupling: float32 [16, 16], replicated, may hold values from -15 to 15
- stick_column: int32 [2048], replicated, may hold values from 0 to 20735, as said below
- stick_heights: int32 [144, 2048], P(None, 'fft'), may hold values from 0 to 287, as said below
- projector_atom: int32 [16], replicated, may hold values from 0 to 3, never falling along the last dimension, each value on 1 to 8 neighbouring positions
Outputs:
- applied_h: float32 [2, 4, 144, 2048], P(None, 'band', None, 'fft')
- projections: float32 [2, 16, 4], P(None, None, 'band')
- subspace: float32 [2, 4, 4], replicated
The draws below stay inside these ranges and needn't reach their ends.
Inputs may be any that keep to these rules, and one draw needn't show every extreme that they name: `stick_column`: the sticks name distinct grid points; points 0 and 20735 are always among them. `stick_heights`: the 144 slots of each stick name distinct heights. `projector_atom`: never falls along the projectors; every atom has 1 to 8 projectors.
All inputs are finite; a program needn't handle non-finite values.
Results may differ from the reference program's by a relative error of at most 0.000073.
Values sent between devices are 32-bit elements; how exact they have to be, the bound alone decides.
A program may use at most 192 MiB of HBM per device.

```python
import math
import jax
import jax.numpy as jnp
import numpy as np
from jax import lax

NX = 144
NY = 144
NZ = 288
SZ = 144
NPROJ = 16
NATOM = 4
NSTICK = 2048
BANDS = 4


def draw_orbitals(key, part):
    key_pattern = jax.random.fold_in(key, 101)
    key_weight = jax.random.fold_in(key, 202)
    key_residue = jax.random.fold_in(key, 303)
    patterns = jax.random.truncated_normal(key_pattern, -4.0, 4.0, (4, 2, SZ, NSTICK), jnp.float32)
    weights = 0.5 * jax.random.truncated_normal(key_weight, -3.0, 3.0, (4, BANDS), jnp.float32)
    residue = 0.7 * jax.random.truncated_normal(key_residue, -4.0, 4.0, (2, BANDS, SZ, NSTICK), jnp.float32)
    mixture = residue
    for member in range(4):
        mixture = mixture + weights[member][None, :, None, None] * patterns[member][:, None]
    return mixture.astype(jnp.float32)


def draw_stick_column(key, part):
    cell_count = NX * NY
    scores = jax.random.randint(key, (cell_count,), 0, 65536, dtype=jnp.int32) * cell_count + jnp.arange(cell_count, dtype=jnp.int32)
    scores = scores.at[0].set(-2).at[cell_count - 1].set(-1)
    ordering = jnp.argsort(scores, stable=True)
    return ordering[:NSTICK].astype(jnp.int32)


def draw_stick_heights(key, part):
    scores = jax.random.randint(key, (NZ, NSTICK), 0, 1 << 20, dtype=jnp.int32) * NZ + jnp.arange(NZ, dtype=jnp.int32)[:, None]
    ordering = jnp.argsort(scores, axis=0, stable=True)
    return ordering[:SZ].astype(jnp.int32)


def steps_of(key, extent, pieces, smallest, largest):
    factor_of = 1.0
    for dim, shards_of in pieces:
        heights = jax.random.uniform(jax.random.fold_in(jax.random.fold_in(key, 6), dim), (shards_of,), jnp.float32, smallest / len(pieces), largest / len(pieces))
        factor_of = factor_of * jnp.repeat(jnp.exp(heights), extent[dim] // shards_of).reshape((-1,) + (1,) * (len(extent) - 1 - dim))
    return factor_of


def length_profile(count, total, limit, lean):
    portions = [(1 << 20) // math.isqrt(standing ** lean) + 1 for standing in range(2, count + 1)]
    rest, given = total - limit - (count - 1), [1] * (count - 1)
    while rest > 0:
        free = [i for i in range(count - 1) if given[i] < limit]
        mass, remaining = sum([portions[i] for i in free]), rest
        for i in free:
            addition = min(limit - given[i], max(1, remaining * portions[i] // mass), rest)
            given[i] = given[i] + addition
            rest = rest - addition
    return np.array([limit] + given)


def ragged(key, number_of, total, reach, slope):
    if number_of == 2:
        one = jax.random.randint(key, (), max(1, total - reach), min(reach, total - 1) + 1)
        return jnp.stack([one, total - one])
    lengths = jnp.asarray(length_profile(number_of, total, reach, slope), jnp.int32)
    twos = (number_of - 1) // 2
    source_of, sink = lengths[1:1 + 2 * twos:2], lengths[2:2 + 2 * twos:2]
    margin = jnp.minimum(source_of - 1, reach - sink)
    passed = jax.random.randint(jax.random.fold_in(key, 1), (twos,), 0, 1 << 20) % (margin + 1)
    lengths = lengths.at[1:1 + 2 * twos:2].set(source_of - passed).at[2:2 + 2 * twos:2].set(sink + passed)
    return lengths[jax.random.permutation(jax.random.fold_in(key, 2), number_of)]


def bell_draw(stream_key, extent, scale, bound, split=(), kind=jnp.bfloat16):
    values = scale * jax.random.normal(stream_key, extent, jnp.float32)
    if split:
        values = values * steps_of(stream_key, extent, split, -0.22, 0.18)
    return jnp.clip(values, -bound, bound).astype(kind)


def setup_inputs(seed: int = 0) -> dict:
    seeds = jax.random.split(jax.random.key(seed), 8)
    return {
        "orbitals": draw_orbitals(jax.random.fold_in(seeds[7], 71), 0),
        "potential": jnp.clip(-3.0 + 4.0 * jax.random.uniform(seeds[1], (NZ, NX * NY), jnp.float32) ** steps_of(seeds[1], (NZ, NX * NY), ((0, 8),), -0.2, 0.2), -3.0, 1.0),
        "projectors": bell_draw(seeds[2], (2, NPROJ, SZ, NSTICK), 1.0, 6.0, ((3, 8),), jnp.float32),
        "coupling": bell_draw(seeds[3], (NPROJ, NPROJ), 3.0, 15.0, (), jnp.float32),
        "stick_column": draw_stick_column(jax.random.fold_in(seeds[7], 71), 0),
        "stick_heights": draw_stick_heights(jax.random.fold_in(seeds[7], 71), 0),
        "projector_atom": jnp.searchsorted(jnp.cumsum(ragged(seeds[6], NATOM, NPROJ, 8, 0)), jnp.arange(NPROJ), side="right").astype(jnp.int32),
    }


KINETIC = 8.0
HIGHEST = lax.Precision.HIGHEST

def frequency(position, length):
    return jnp.where(position < (length + 1) // 2, position, position - length).astype(jnp.float32)

def conj_pairs(left, right):
    blocks = jnp.einsum('pmgs,qngs->pqmn', left, right, precision=HIGHEST)
    return jnp.stack([blocks[0, 0] + blocks[1, 1], blocks[0, 1] - blocks[1, 0]], 0)

def reference(orbitals, potential, projectors, coupling, stick_column, stick_heights, projector_atom):
    plane_points = NX * NY
    grid_total = NX * NY * NZ
    coeff_total = NSTICK * SZ
    along_x = frequency(stick_column // NY, NX) / NX
    along_y = frequency(stick_column % NY, NY) / NY
    along_z = frequency(stick_heights, NZ) / NZ
    kinetic = KINETIC * (along_x * along_x + along_y * along_y)[None, :] + KINETIC * along_z * along_z
    places = (stick_heights * plane_points + stick_column[None, :]).reshape(-1).astype(jnp.int32)
    potential_grid = potential.reshape(NZ, NX, NY)

    def apply_local(pair):
        dense_real = jnp.zeros((grid_total,), jnp.float32).at[places].set(pair[0].reshape(-1))
        dense_imag = jnp.zeros((grid_total,), jnp.float32).at[places].set(pair[1].reshape(-1))
        spectrum = lax.complex(dense_real, dense_imag).reshape(NZ, NX, NY)
        spatial = jnp.fft.ifftn(spectrum) * grid_total
        product = spatial * potential_grid
        back = jnp.fft.fftn(product).reshape(-1)[places] / grid_total
        return jnp.stack([jnp.real(back).reshape(SZ, NSTICK), jnp.imag(back).reshape(SZ, NSTICK)], 0)
    local_term = jnp.moveaxis(lax.map(apply_local, jnp.moveaxis(orbitals, 1, 0)), 0, 1)
    norm_scale = 1.0 / math.sqrt(coeff_total)
    raw_products = jnp.einsum('pkgs,qbgs->pqkb', projectors, orbitals, precision=HIGHEST)
    projections = jnp.stack([raw_products[0, 0] + raw_products[1, 1], raw_products[0, 1] - raw_products[1, 0]], 0) * norm_scale
    same_atom = projector_atom[:, None] == projector_atom[None, :]
    atom_coupling = jnp.where(same_atom, 0.5 * (coupling + coupling.T), jnp.zeros_like(coupling))
    weighted = jnp.einsum('kl,plb->pkb', atom_coupling, projections, precision=HIGHEST)
    spread = jnp.einsum('pkgs,qkb->pqbgs', projectors, weighted, precision=HIGHEST)
    nonlocal_term = jnp.stack([spread[0, 0] - spread[1, 1], spread[0, 1] + spread[1, 0]], 0) * norm_scale
    applied_h = kinetic * orbitals + local_term + nonlocal_term
    subspace = conj_pairs(orbitals, applied_h) / coeff_total
    return (applied_h, projections, subspace)
```

```python
import functools
import math

import jax
import jax.numpy as jnp
import ml_dtypes
import numpy as np
from jax import lax
from jax.experimental import pallas as pl
from jax.experimental.pallas import tpu as pltpu
from jax.sharding import PartitionSpec as P

NX = 144
NY = 144
NZ = 288
HALF = 64
LANES = 128
KINETIC = 8.0
HIGHEST = lax.Precision.HIGHEST
F32 = jnp.float32
BF16 = jnp.bfloat16


def frequency(position, length):
    return jnp.where(position < (length + 1) // 2, position, position - length).astype(F32)


def angles(rows, columns, length):
    phase = np.outer(np.arange(rows), np.arange(columns)) % length
    return 2.0 * np.pi / length * phase


def split_table(table):
    high = table.astype(np.float32).astype(ml_dtypes.bfloat16)
    low = (table - high.astype(np.float64)).astype(np.float32).astype(ml_dtypes.bfloat16)
    return high, low


def plane_table(length):
    angle = angles(length, length, length)
    return split_table(np.concatenate([np.cos(angle), np.sin(angle)], 0))


def normal_tables(devices, planes, padded):
    angle = angles(NZ, NZ, NZ)
    cosine, sine = np.cos(angle), np.sin(angle)
    forward = np.zeros((devices, 2, padded, 2, NZ))
    forward[:, 0, :planes, 0] = cosine.reshape(devices, planes, NZ)
    forward[:, 0, :planes, 1] = -sine.reshape(devices, planes, NZ)
    forward[:, 1, :planes, 0] = sine.reshape(devices, planes, NZ)
    forward[:, 1, :planes, 1] = cosine.reshape(devices, planes, NZ)
    forward = forward.reshape(devices * 2 * padded, 2 * NZ)
    return split_table(forward), split_table(forward.T.copy())


def split_value(value):
    high = value.astype(BF16)
    low = (value - high.astype(F32)).astype(BF16)
    return high, low


def dot3(table_high, table_low, value):
    high, low = split_value(value)
    dot = functools.partial(jnp.dot, preferred_element_type=F32)
    return dot(table_high, high) + dot(table_low, high) + dot(table_high, low)


def projection_kernel(projector_ref, orbital_ref, out_ref):
    pr, pi = projector_ref[0, 0], projector_ref[1, 0]
    orb_r, orb_i = orbital_ref[0, 0], orbital_ref[1, 0]
    out_ref[0, 0:1, :] = jnp.sum(pr * orb_r + pi * orb_i, axis=0, keepdims=True)
    out_ref[0, 1:2, :] = jnp.sum(pr * orb_i - pi * orb_r, axis=0, keepdims=True)


def normal_kernel(planes, orbital_ref, height_ref, high_ref, low_ref, out_ref, dense, slot_heights, slot_values):
    slots, sticks = height_ref.shape
    block = NZ // 2
    base = lax.broadcasted_iota(jnp.int32, (block, LANES), 0)
    for lane in range(0, sticks, LANES):
        slot_heights[...] = height_ref[:, lane : lane + LANES]
        slot_values[0] = orbital_ref[0, 0, :, lane : lane + LANES]
        slot_values[1] = orbital_ref[1, 0, :, lane : lane + LANES]
        for start in range(0, NZ, block):

            def step(slot, carry):
                real, imag = carry
                here = base + start == slot_heights[pl.ds(slot, 1), :]
                row_r = slot_values[0, pl.ds(slot, 1), :]
                row_i = slot_values[1, pl.ds(slot, 1), :]
                return jnp.where(here, row_r, real), jnp.where(here, row_i, imag)

            zero = jnp.zeros((block, LANES), F32)
            real, imag = lax.fori_loop(0, slots, step, (zero, zero), unroll=4)
            dense[start : start + block, lane : lane + LANES] = real
            dense[NZ + start : NZ + start + block, lane : lane + LANES] = imag
    result = dot3(high_ref[...], low_ref[...], dense[...])
    devices = out_ref.shape[0]
    padded = result.shape[0] // (2 * devices)
    for device in range(devices):
        for part in range(2):
            first = (device * 2 + part) * padded
            out_ref[device, part] = result[first : first + planes]


def plane_kernel(
    column_ref, received_ref, potential_ref, high_ref, low_ref, out_ref, grid, factor, wide, tall, rows
):
    devices, _, planes, sticks = received_ref.shape
    total = devices * sticks
    points = NX * NY
    lane = lax.broadcasted_iota(jnp.int32, (1, LANES), 1)
    sign = jnp.where(lane < HALF, -1.0, 1.0).astype(F32)

    tall[...] = jnp.zeros_like(tall)
    tall[0:planes, :] = potential_ref[...]

    def lay(index, carry):
        at = pl.ds(pl.multiple_of(index * LANES, LANES), LANES)
        piece = tall[:, at]
        factor[at, :] = jnp.concatenate([piece, piece], 0).T
        return carry

    lax.fori_loop(0, points // LANES, lay, 0, unroll=2)

    wide[...] = jnp.zeros_like(wide)
    for device in range(devices):
        for part in range(2):
            wide[part * HALF : part * HALF + planes, device * sticks : (device + 1) * sticks] = (
                received_ref[device, part]
            )
    for first in range(0, total, LANES):
        rows[first : first + LANES, :] = wide[:, first : first + LANES].T

    def clear(index, carry):
        grid[pl.ds(pl.multiple_of(index * NY, 8), NY), :] = jnp.zeros((NY, LANES), F32)
        return carry

    lax.fori_loop(0, NX, clear, 0)

    def put(stick, carry):
        grid[pl.ds(column_ref[stick], 1), :] = rows[pl.ds(stick, 1), :]
        return carry

    lax.fori_loop(0, total, put, 0, unroll=8)

    def transform(value, direction):
        product = dot3(high_ref[...], low_ref[...], value)
        length = product.shape[0] // 2
        turned = [
            product[:length, i : i + LANES]
            + (direction * sign) * pltpu.roll(product[length:, i : i + LANES], HALF, 1)
            for i in range(0, 2 * LANES, LANES)
        ]
        return turned

    def along_y(direction):
        def step(pair, carry):
            first = pl.ds(pl.multiple_of(pair * 2 * NY, 8), NY)
            second = pl.ds(pl.multiple_of((pair * 2 + 1) * NY, 8), NY)
            left, right = transform(jnp.concatenate([grid[first, :], grid[second, :]], 1), direction)
            grid[first, :] = left
            grid[second, :] = right
            return carry

        lax.fori_loop(0, NX // 2, step, 0)

    def along_x(pair, carry):
        first = pl.ds(pair * 2, NX, stride=NY)
        second = pl.ds(pair * 2 + 1, NX, stride=NY)
        left, right = transform(jnp.concatenate([grid[first, :], grid[second, :]], 1), 1.0)
        left = left * factor[first, :]
        right = right * factor[second, :]
        left, right = transform(jnp.concatenate([left, right], 1), -1.0)
        grid[first, :] = left
        grid[second, :] = right
        return carry

    along_y(1.0)
    lax.fori_loop(0, NY // 2, along_x, 0)
    along_y(-1.0)

    def take(stick, carry):
        rows[pl.ds(stick, 1), :] = grid[pl.ds(column_ref[stick], 1), :]
        return carry

    lax.fori_loop(0, total, take, 0, unroll=8)
    for first in range(0, total, LANES):
        device, start = first // sticks, first % sticks
        piece = rows[first : first + LANES, :].T
        for part in range(2):
            out_ref[device, part, :, start : start + LANES] = piece[
                part * HALF : part * HALF + planes
            ]


def final_kernel(
    weight_ref,
    back_ref,
    high_ref,
    low_ref,
    height_ref,
    plane_kinetic_ref,
    orbital_ref,
    projector_ref,
    all_ref,
    out_ref,
    sum_ref,
    packed,
    spectrum,
):
    devices, _, planes, sticks = back_ref.shape
    padded = packed.shape[0] // (2 * devices)
    slots = height_ref.shape[0]
    projector_count = projector_ref.shape[1]
    band_total = all_ref.shape[1]
    grid_total = NX * NY * NZ
    packed[...] = jnp.zeros_like(packed)
    for device in range(devices):
        for part in range(2):
            first = (device * 2 + part) * padded
            packed[first : first + planes, :] = back_ref[device, part]
    result = dot3(high_ref[...], low_ref[...], packed[...])
    for lane in range(0, sticks, LANES):
        spectrum[lane // LANES] = result[:, lane : lane + LANES]
    for lane in range(0, sticks, LANES):
        lanes = slice(lane, lane + LANES)
        heights = height_ref[:, lanes]

        def step(height, carry):
            real, imag = carry
            here = heights == height
            row_r = spectrum[lane // LANES, pl.ds(height, 1), :]
            row_i = spectrum[lane // LANES, pl.ds(NZ + height, 1), :]
            return jnp.where(here, row_r, real), jnp.where(here, row_i, imag)

        zero = jnp.zeros((slots, LANES), F32)
        real, imag = lax.fori_loop(0, NZ, step, (zero, zero), unroll=4)
        out_ref[0, 0, :, lanes] = real / grid_total
        out_ref[1, 0, :, lanes] = imag / grid_total
    row_count = 48
    for first in range(0, slots, row_count):
        at = slice(first, first + row_count)
        for lane in range(0, sticks, LANES):
            lanes = slice(lane, lane + LANES)
            along_z = frequency(height_ref[at, lanes], NZ) / NZ
            kinetic = plane_kinetic_ref[:, lanes] + KINETIC * along_z * along_z
            real = jnp.zeros((row_count, LANES), F32)
            imag = jnp.zeros((row_count, LANES), F32)
            for k in range(projector_count):
                pr = projector_ref[0, k, at, lanes]
                pi = projector_ref[1, k, at, lanes]
                wr, wi = weight_ref[0, k], weight_ref[1, k]
                real = real + (pr * wr - pi * wi)
                imag = imag + (pr * wi + pi * wr)
            out_ref[0, 0, at, lanes] = (
                kinetic * orbital_ref[0, 0, at, lanes] + out_ref[0, 0, at, lanes] + real
            )
            out_ref[1, 0, at, lanes] = (
                kinetic * orbital_ref[1, 0, at, lanes] + out_ref[1, 0, at, lanes] + imag
            )
    for band in range(band_total):
        hr, hi = out_ref[0, 0], out_ref[1, 0]
        br, bi = all_ref[0, band], all_ref[1, band]
        sum_ref[0, band : band + 1, :] = jnp.sum(br * hr + bi * hi, axis=0, keepdims=True)
        sum_ref[1, band : band + 1, :] = jnp.sum(br * hi - bi * hr, axis=0, keepdims=True)


def params(mebibytes):
    return pltpu.CompilerParams(vmem_limit_bytes=mebibytes << 20)


def body(orbitals, potential, projectors, coupling, stick_column, stick_heights, projector_atom):
    slot_count = orbitals.shape[2]
    sticks_here = orbitals.shape[3]
    projector_count = projectors.shape[1]
    planes_here = potential.shape[0]
    devices = NZ // planes_here
    stick_total = stick_column.shape[0]
    coeff_total = slot_count * stick_total
    padded = -(-planes_here // 8) * 8
    packed_rows = devices * 2 * padded
    vmem = pl.BlockSpec(memory_space=pltpu.VMEM)
    smem = pl.BlockSpec(memory_space=pltpu.SMEM)
    (z_high, z_low), (back_high, back_low) = normal_tables(devices, planes_here, padded)
    plane_high, plane_low = plane_table(NX)

    all_orbitals = lax.all_gather(orbitals, "band", axis=1, tiled=True)
    band_total = all_orbitals.shape[1]
    first_stick = lax.axis_index("fft") * sticks_here
    local_columns = lax.dynamic_slice_in_dim(stick_column, first_stick, sticks_here)
    along_x = frequency(local_columns // NY, NX) / NX
    along_y = frequency(local_columns % NY, NY) / NY
    plane_kinetic = (KINETIC * (along_x * along_x + along_y * along_y))[None, :]

    block = (2, 1, slot_count, sticks_here)
    partial = pl.pallas_call(
        projection_kernel,
        grid=(projector_count,),
        in_specs=[
            pl.BlockSpec(block, lambda k: (0, k, 0, 0)),
            pl.BlockSpec(block, lambda k: (0, 0, 0, 0)),
        ],
        out_specs=pl.BlockSpec((1, 2, sticks_here), lambda k: (k, 0, 0)),
        out_shape=jax.ShapeDtypeStruct((projector_count, 2, sticks_here), F32),
        compiler_params=params(16),
        cost_estimate=pl.CostEstimate(flops=5000000, bytes_accessed=5000000, transcendentals=0),
    )(projectors, orbitals)
    norm_scale = 1.0 / math.sqrt(coeff_total)
    partial = jnp.sum(partial, axis=2).T[:, :, None]
    projections = lax.psum(partial, "fft") * norm_scale
    same_atom = projector_atom[:, None] == projector_atom[None, :]
    atom_coupling = jnp.where(same_atom, 0.5 * (coupling + coupling.T), jnp.zeros_like(coupling))
    weighted = jnp.einsum("kl,plb->pkb", atom_coupling, projections, precision=HIGHEST)

    exchange = (devices, 2, planes_here, sticks_here)
    z_space = pl.pallas_call(
        functools.partial(normal_kernel, planes_here),
        in_specs=[vmem] * 4,
        out_specs=vmem,
        out_shape=jax.ShapeDtypeStruct(exchange, F32),
        scratch_shapes=[
            pltpu.VMEM((2 * NZ, sticks_here), F32),
            pltpu.VMEM((slot_count, LANES), jnp.int32),
            pltpu.VMEM((2, slot_count, LANES), F32),
        ],
        compiler_params=params(24),
        cost_estimate=pl.CostEstimate(flops=600000000, bytes_accessed=3000000, transcendentals=0),
    )(orbitals, stick_heights, z_high, z_low)
    received = lax.all_to_all(z_space, "fft", split_axis=0, concat_axis=0, tiled=True)
    values = pl.pallas_call(
        plane_kernel,
        in_specs=[smem] + [vmem] * 4,
        out_specs=vmem,
        out_shape=jax.ShapeDtypeStruct(exchange, F32),
        scratch_shapes=[
            pltpu.VMEM((NX * NY, LANES), F32),
            pltpu.VMEM((NX * NY, LANES), F32),
            pltpu.VMEM((2 * HALF, stick_total), F32),
            pltpu.VMEM((HALF, NX * NY), F32),
            pltpu.VMEM((stick_total, LANES), F32),
        ],
        compiler_params=params(56),
        cost_estimate=pl.CostEstimate(
            flops=60000000000, bytes_accessed=6000000, transcendentals=0
        ),
    )(stick_column, received, potential, plane_high, plane_low)
    results = lax.all_to_all(values, "fft", split_axis=0, concat_axis=0, tiled=True)
    applied_h, sums = pl.pallas_call(
        final_kernel,
        in_specs=[smem] + [vmem] * 8,
        out_specs=(vmem, vmem),
        out_shape=(
            jax.ShapeDtypeStruct(orbitals.shape, F32),
            jax.ShapeDtypeStruct((2, band_total, sticks_here), F32),
        ),
        scratch_shapes=[
            pltpu.VMEM((packed_rows, sticks_here), F32),
            pltpu.VMEM((sticks_here // LANES, 2 * NZ, LANES), F32),
        ],
        compiler_params=params(40),
        cost_estimate=pl.CostEstimate(flops=600000000, bytes_accessed=9000000, transcendentals=0),
    )(
        weighted[:, :, 0] * norm_scale,
        results,
        back_high,
        back_low,
        stick_heights,
        plane_kinetic,
        orbitals,
        projectors,
        all_orbitals,
    )
    column = jnp.sum(sums, axis=2)[:, :, None]
    mine = jnp.arange(band_total) == lax.axis_index("band")
    spread = jnp.where(mine[None, None, :], column, jnp.zeros_like(column))
    subspace = lax.psum(spread, ("band", "fft")) / coeff_total
    return (applied_h, projections, subspace)


def solution(mesh):
    in_specs = (
        P(None, "band", None, "fft"),
        P("fft", None),
        P(None, None, None, "fft"),
        P(),
        P(),
        P(None, "fft"),
        P(),
    )
    out_specs = (P(None, "band", None, "fft"), P(None, None, "band"), P())
    return jax.shard_map(body, mesh=mesh, in_specs=in_specs, out_specs=out_specs, check_vma=False)
```

```python
import functools
import math

import jax
import jax.numpy as jnp
import ml_dtypes
import numpy as np
from jax import lax
from jax.experimental import pallas as pl
from jax.experimental.pallas import tpu as pltpu
from jax.sharding import PartitionSpec as P

NX = 144
NY = 144
NZ = 288
HALF = 64
LANES = 128
KINETIC = 8.0
HIGHEST = lax.Precision.HIGHEST
F32 = jnp.float32
BF16 = jnp.bfloat16
MESH = pl.DeviceIdType.MESH


def frequency(position, length):
    return jnp.where(position < (length + 1) // 2, position, position - length).astype(F32)


def angles(rows, columns, length):
    phase = np.outer(np.arange(rows), np.arange(columns)) % length
    return 2.0 * np.pi / length * phase


def split_table(table):
    high = table.astype(np.float32).astype(ml_dtypes.bfloat16)
    low = (table - high.astype(np.float64)).astype(np.float32).astype(ml_dtypes.bfloat16)
    return high, low


def plane_table(length):
    angle = angles(length, length, length)
    return split_table(np.concatenate([np.cos(angle), np.sin(angle)], 0))


def normal_tables(devices, planes, padded):
    angle = angles(NZ, NZ, NZ)
    cosine, sine = np.cos(angle), np.sin(angle)
    forward = np.zeros((devices, 2, padded, 2, NZ))
    forward[:, 0, :planes, 0] = cosine.reshape(devices, planes, NZ)
    forward[:, 0, :planes, 1] = -sine.reshape(devices, planes, NZ)
    forward[:, 1, :planes, 0] = sine.reshape(devices, planes, NZ)
    forward[:, 1, :planes, 1] = cosine.reshape(devices, planes, NZ)
    forward = forward.reshape(devices * 2 * padded, 2 * NZ)
    return split_table(forward), split_table(forward.T.copy())


def split_value(value):
    high = value.astype(BF16)
    low = (value - high.astype(F32)).astype(BF16)
    return high, low


def dot3(table_high, table_low, value):
    high, low = split_value(value)
    dot = functools.partial(jnp.dot, preferred_element_type=F32)
    return dot(table_high, high) + dot(table_low, high) + dot(table_high, low)


def fold(row):
    return sum(row[:, i : i + LANES] for i in range(0, row.shape[1], LANES))


def normal_kernel(
    planes,
    orbital_ref,
    height_ref,
    high_ref,
    low_ref,
    projector_ref,
    out_ref,
    dense,
    slot_heights,
    slot_values,
    held,
    partial,
    arrived,
):
    slots, sticks = height_ref.shape
    projector_count = projector_ref.shape[1]
    fetch = pltpu.make_async_copy(projector_ref, held, arrived)
    fetch.start()
    block = NZ // 2
    base = lax.broadcasted_iota(jnp.int32, (block, LANES), 0)
    for lane in range(0, sticks, LANES):
        slot_heights[...] = height_ref[:, lane : lane + LANES]
        slot_values[0] = orbital_ref[0, 0, :, lane : lane + LANES]
        slot_values[1] = orbital_ref[1, 0, :, lane : lane + LANES]
        for start in range(0, NZ, block):

            def step(slot, carry):
                real, imag = carry
                here = base + start == slot_heights[pl.ds(slot, 1), :]
                row_r = slot_values[0, pl.ds(slot, 1), :]
                row_i = slot_values[1, pl.ds(slot, 1), :]
                return jnp.where(here, row_r, real), jnp.where(here, row_i, imag)

            zero = jnp.zeros((block, LANES), F32)
            real, imag = lax.fori_loop(0, slots, step, (zero, zero), unroll=4)
            dense[start : start + block, lane : lane + LANES] = real
            dense[NZ + start : NZ + start + block, lane : lane + LANES] = imag
    result = dot3(high_ref[...], low_ref[...], dense[...])
    devices = out_ref.shape[0]
    padded = result.shape[0] // (2 * devices)
    for device in range(devices):
        for part in range(2):
            first = (device * 2 + part) * padded
            out_ref[device, part * padded : (part + 1) * padded, :] = result[
                first : first + padded
            ]
    fetch.wait()
    partial[...] = jnp.zeros_like(partial)
    orb_r, orb_i = orbital_ref[0, 0], orbital_ref[1, 0]
    for k in range(projector_count):
        pr, pi = held[0, k], held[1, k]
        real = jnp.sum(pr * orb_r + pi * orb_i, axis=0, keepdims=True)
        imag = jnp.sum(pr * orb_i - pi * orb_r, axis=0, keepdims=True)
        partial[k : k + 1, :] = fold(real)
        partial[HALF + k : HALF + k + 1, :] = fold(imag)
    sums = jnp.sum(partial[...].T, axis=0, keepdims=True)
    sums = jnp.concatenate([sums] + [jnp.zeros_like(sums)] * (sticks // LANES - 1), 1)
    sums = jnp.broadcast_to(sums, (8, sticks))
    for device in range(devices):
        out_ref[device, 2 * padded :, :] = sums


def plane_kernel(
    column_ref, received_ref, potential_ref, table_ref, out_ref, total_ref, grid, factor, wide, tall, rows
):
    devices, _, sticks = received_ref.shape
    planes = potential_ref.shape[0]
    padded = (received_ref.shape[1] - 8) // 2
    total = devices * sticks
    points = NX * NY
    lane = lax.broadcasted_iota(jnp.int32, (1, LANES), 1)
    sign = jnp.where(lane < HALF, -1.0, 1.0).astype(F32)

    tall[...] = jnp.zeros_like(tall)
    tall[0:planes, :] = potential_ref[...]

    def lay(index, carry):
        at = pl.ds(pl.multiple_of(index * LANES, LANES), LANES)
        piece = tall[:, at]
        factor[at, :] = jnp.concatenate([piece, piece], 0).T
        return carry

    lax.fori_loop(0, points // LANES, lay, 0, unroll=9)

    wide[...] = jnp.zeros_like(wide)
    for device in range(devices):
        for part in range(2):
            wide[part * HALF : part * HALF + padded, device * sticks : (device + 1) * sticks] = (
                received_ref[device, part * padded : (part + 1) * padded, :]
            )
    total_ref[...] = sum(received_ref[device, 2 * padded :, 0:LANES] for device in range(devices))
    for first in range(0, total, LANES):
        rows[first : first + LANES, :] = wide[:, first : first + LANES].T

    def clear(index, carry):
        grid[pl.ds(pl.multiple_of(index * NY, 8), NY), :] = jnp.zeros((NY, LANES), F32)
        return carry

    lax.fori_loop(0, NX, clear, 0, unroll=4)

    def put(stick, carry):
        grid[pl.ds(column_ref[stick], 1), :] = rows[pl.ds(stick, 1), :]
        return carry

    lax.fori_loop(0, total, put, 0, unroll=16)

    def transform(value, direction):
        high, low = split_value(value)
        product = jnp.dot(
            table_ref[...], jnp.concatenate([high, low, high], 0), preferred_element_type=F32
        )
        length = product.shape[0] // 2
        turned = [
            product[:length, i : i + LANES]
            + (direction * sign) * pltpu.roll(product[length:, i : i + LANES], HALF, 1)
            for i in range(0, 2 * LANES, LANES)
        ]
        return turned

    def along_y(direction):
        def step(pair, carry):
            first = pl.ds(pl.multiple_of(pair * 2 * NY, 8), NY)
            second = pl.ds(pl.multiple_of((pair * 2 + 1) * NY, 8), NY)
            left, right = transform(jnp.concatenate([grid[first, :], grid[second, :]], 1), direction)
            grid[first, :] = left
            grid[second, :] = right
            return carry

        lax.fori_loop(0, NX // 2, step, 0, unroll=6)

    def along_x(pair, carry):
        first = pl.ds(pair * 2, NX, stride=NY)
        second = pl.ds(pair * 2 + 1, NX, stride=NY)
        left, right = transform(jnp.concatenate([grid[first, :], grid[second, :]], 1), 1.0)
        left = left * factor[first, :]
        right = right * factor[second, :]
        left, right = transform(jnp.concatenate([left, right], 1), -1.0)
        grid[first, :] = left
        grid[second, :] = right
        return carry

    along_y(1.0)
    lax.fori_loop(0, NY // 2, along_x, 0, unroll=6)
    along_y(-1.0)

    def take(stick, carry):
        rows[pl.ds(stick, 1), :] = grid[pl.ds(column_ref[stick], 1), :]
        return carry

    lax.fori_loop(0, total, take, 0, unroll=8)
    for first in range(0, total, LANES):
        device, start = first // sticks, first % sticks
        piece = rows[first : first + LANES, :].T
        for part in range(2):
            out_ref[device, part * padded : (part + 1) * padded, start : start + LANES] = piece[
                part * HALF : part * HALF + padded
            ]


def final_kernel(
    weight_ref,
    back_ref,
    high_ref,
    low_ref,
    height_ref,
    plane_kinetic_ref,
    orbital_ref,
    projector_ref,
    all_ref,
    out_ref,
    sum_ref,
    spectrum,
):
    devices, double, sticks = back_ref.shape
    padded = double // 2
    slots = height_ref.shape[0]
    projector_count = projector_ref.shape[1]
    band_total = all_ref.shape[1]
    grid_total = NX * NY * NZ
    back = back_ref[...].reshape(devices * 2 * padded, sticks)
    result = dot3(high_ref[...], low_ref[...], back)
    for lane in range(0, sticks, LANES):
        spectrum[lane // LANES] = result[:, lane : lane + LANES]
    for lane in range(0, sticks, LANES):
        lanes = slice(lane, lane + LANES)
        heights = height_ref[:, lanes]

        def step(height, carry):
            real, imag = carry
            here = heights == height
            row_r = spectrum[lane // LANES, pl.ds(height, 1), :]
            row_i = spectrum[lane // LANES, pl.ds(NZ + height, 1), :]
            return jnp.where(here, row_r, real), jnp.where(here, row_i, imag)

        zero = jnp.zeros((slots, LANES), F32)
        real, imag = lax.fori_loop(0, NZ, step, (zero, zero), unroll=4)
        out_ref[0, 0, :, lanes] = real / grid_total
        out_ref[1, 0, :, lanes] = imag / grid_total
    row_count = 48
    for first in range(0, slots, row_count):
        at = slice(first, first + row_count)
        for lane in range(0, sticks, LANES):
            lanes = slice(lane, lane + LANES)
            along_z = frequency(height_ref[at, lanes], NZ) / NZ
            kinetic = plane_kinetic_ref[:, lanes] + KINETIC * along_z * along_z
            real = jnp.zeros((row_count, LANES), F32)
            imag = jnp.zeros((row_count, LANES), F32)
            for k in range(projector_count):
                pr = projector_ref[0, k, at, lanes]
                pi = projector_ref[1, k, at, lanes]
                wr, wi = weight_ref[0, k], weight_ref[1, k]
                real = real + (pr * wr - pi * wi)
                imag = imag + (pr * wi + pi * wr)
            out_ref[0, 0, at, lanes] = (
                kinetic * orbital_ref[0, 0, at, lanes] + out_ref[0, 0, at, lanes] + real
            )
            out_ref[1, 0, at, lanes] = (
                kinetic * orbital_ref[1, 0, at, lanes] + out_ref[1, 0, at, lanes] + imag
            )
    for band in range(band_total):
        hr, hi = out_ref[0, 0], out_ref[1, 0]
        br, bi = all_ref[0, band], all_ref[1, band]
        sum_ref[0, band : band + 1, :] = jnp.sum(br * hr + bi * hi, axis=0, keepdims=True)
        sum_ref[1, band : band + 1, :] = jnp.sum(br * hi - bi * hr, axis=0, keepdims=True)


def gather_kernel(
    fft_count, band_count, sum_ref, out_ref, own, summed, fft_in, band_in, fs, fr, bs, br
):
    fft, band = lax.axis_index("fft"), lax.axis_index("band")
    barrier = pltpu.get_barrier_semaphore()
    for i in range(1, fft_count):
        pl.semaphore_signal(
            barrier, inc=1, device_id=(band, lax.rem(fft + i, fft_count)), device_id_type=MESH
        )
    for i in range(1, band_count):
        pl.semaphore_signal(
            barrier, inc=1, device_id=(lax.rem(band + i, band_count), fft), device_id_type=MESH
        )
    own[...] = fold(sum_ref[...])
    pl.semaphore_wait(barrier, fft_count + band_count - 2)

    def exchange(count, source, slots, send, receive, target):
        copies = []
        for i in range(1, count):
            copy = pltpu.make_async_remote_copy(
                src_ref=source,
                dst_ref=slots.at[i],
                send_sem=send.at[i],
                recv_sem=receive.at[i],
                device_id=target(i),
                device_id_type=MESH,
            )
            copy.start()
            copies.append(copy)
        return copies

    copies = exchange(
        fft_count, own, fft_in, fs, fr, lambda i: (band, lax.rem(fft + i, fft_count))
    )
    for copy in copies:
        copy.wait()
    fft_in[0] = own[...]
    total = jnp.zeros_like(own)
    for i in range(fft_count):
        total = total + fft_in[lax.rem(fft - i + fft_count, fft_count)]
    summed[...] = total
    copies = exchange(
        band_count, summed, band_in, bs, br, lambda i: (lax.rem(band + i, band_count), fft)
    )
    for copy in copies:
        copy.wait()
    band_in[0] = summed[...]
    for i in range(band_count):
        out_ref[i] = band_in[lax.rem(band - i + band_count, band_count)]


def params(mebibytes):
    return pltpu.CompilerParams(vmem_limit_bytes=mebibytes << 20)


def body(orbitals, potential, projectors, coupling, stick_column, stick_heights, projector_atom):
    slot_count = orbitals.shape[2]
    sticks_here = orbitals.shape[3]
    projector_count = projectors.shape[1]
    planes_here = potential.shape[0]
    devices = NZ // planes_here
    stick_total = stick_column.shape[0]
    coeff_total = slot_count * stick_total
    padded = -(-planes_here // 8) * 8
    vmem = pl.BlockSpec(memory_space=pltpu.VMEM)
    smem = pl.BlockSpec(memory_space=pltpu.SMEM)
    (z_high, z_low), (back_high, back_low) = normal_tables(devices, planes_here, padded)
    plane_high, plane_low = plane_table(NX)
    plane_triple = np.concatenate([plane_high, plane_high, plane_low], 1)

    all_orbitals = lax.all_gather(orbitals, "band", axis=1, tiled=True)
    band_total = all_orbitals.shape[1]
    first_stick = lax.axis_index("fft") * sticks_here
    local_columns = lax.dynamic_slice_in_dim(stick_column, first_stick, sticks_here)
    along_x = frequency(local_columns // NY, NX) / NX
    along_y = frequency(local_columns % NY, NY) / NY
    plane_kinetic = (KINETIC * (along_x * along_x + along_y * along_y))[None, :]

    forth = (devices, 2 * padded + 8, sticks_here)
    back = (devices, 2 * padded, sticks_here)
    anywhere = pl.BlockSpec(memory_space=pl.ANY)
    z_space = pl.pallas_call(
        functools.partial(normal_kernel, planes_here),
        in_specs=[vmem] * 4 + [anywhere],
        out_specs=vmem,
        out_shape=jax.ShapeDtypeStruct(forth, F32),
        scratch_shapes=[
            pltpu.VMEM((2 * NZ, sticks_here), F32),
            pltpu.VMEM((slot_count, LANES), jnp.int32),
            pltpu.VMEM((2, slot_count, LANES), F32),
            pltpu.VMEM(projectors.shape, F32),
            pltpu.VMEM((LANES, LANES), F32),
            pltpu.SemaphoreType.DMA,
        ],
        compiler_params=params(24),
        cost_estimate=pl.CostEstimate(flops=600000000, bytes_accessed=3000000, transcendentals=0),
    )(orbitals, stick_heights, z_high, z_low, projectors)
    received = lax.all_to_all(z_space, "fft", split_axis=0, concat_axis=0, tiled=True)
    values, total = pl.pallas_call(
        plane_kernel,
        in_specs=[smem] + [vmem] * 3,
        out_specs=(vmem, vmem),
        out_shape=(jax.ShapeDtypeStruct(back, F32), jax.ShapeDtypeStruct((8, LANES), F32)),
        scratch_shapes=[
            pltpu.VMEM((NX * NY, LANES), F32),
            pltpu.VMEM((NX * NY, LANES), F32),
            pltpu.VMEM((2 * HALF, stick_total), F32),
            pltpu.VMEM((HALF, NX * NY), F32),
            pltpu.VMEM((stick_total, LANES), F32),
        ],
        compiler_params=params(56),
        cost_estimate=pl.CostEstimate(
            flops=60000000000, bytes_accessed=6000000, transcendentals=0
        ),
    )(stick_column, received, potential, plane_triple)
    norm_scale = 1.0 / math.sqrt(coeff_total)
    total = total[0].reshape(2, HALF)[:, :projector_count, None]
    projections = total * norm_scale
    same_atom = projector_atom[:, None] == projector_atom[None, :]
    atom_coupling = jnp.where(same_atom, 0.5 * (coupling + coupling.T), jnp.zeros_like(coupling))
    weighted = jnp.einsum("kl,plb->pkb", atom_coupling, projections, precision=HIGHEST)
    results = lax.all_to_all(values, "fft", split_axis=0, concat_axis=0, tiled=True)
    applied_h, sums = pl.pallas_call(
        final_kernel,
        in_specs=[smem] + [vmem] * 8,
        out_specs=(vmem, vmem),
        out_shape=(
            jax.ShapeDtypeStruct(orbitals.shape, F32),
            jax.ShapeDtypeStruct((2, band_total, sticks_here), F32),
        ),
        scratch_shapes=[
            pltpu.VMEM((sticks_here // LANES, 2 * NZ, LANES), F32),
        ],
        compiler_params=params(40),
        cost_estimate=pl.CostEstimate(flops=600000000, bytes_accessed=9000000, transcendentals=0),
    )(
        weighted[:, :, 0] * norm_scale,
        results,
        back_high,
        back_low,
        stick_heights,
        plane_kinetic,
        orbitals,
        projectors,
        all_orbitals,
    )
    band_devices = band_total // orbitals.shape[1]
    rows = 2 * band_total
    gathered = pl.pallas_call(
        functools.partial(gather_kernel, devices, band_devices),
        in_specs=[vmem],
        out_specs=vmem,
        out_shape=jax.ShapeDtypeStruct((band_devices, rows, LANES), F32),
        scratch_shapes=[
            pltpu.VMEM((rows, LANES), F32),
            pltpu.VMEM((rows, LANES), F32),
            pltpu.VMEM((devices, rows, LANES), F32),
            pltpu.VMEM((band_devices, rows, LANES), F32),
            pltpu.SemaphoreType.DMA((devices,)),
            pltpu.SemaphoreType.DMA((devices,)),
            pltpu.SemaphoreType.DMA((band_devices,)),
            pltpu.SemaphoreType.DMA((band_devices,)),
        ],
        compiler_params=pltpu.CompilerParams(collective_id=0, has_side_effects=True),
    )(sums.reshape(rows, sticks_here))
    subspace = jnp.sum(gathered, axis=2).reshape(band_devices, 2, band_total)
    subspace = jnp.transpose(subspace, (1, 2, 0)) / coeff_total
    return (applied_h, projections, subspace)


def solution(mesh):
    in_specs = (
        P(None, "band", None, "fft"),
        P("fft", None),
        P(None, None, None, "fft"),
        P(),
        P(),
        P(None, "fft"),
        P(),
    )
    out_specs = (P(None, "band", None, "fft"), P(None, None, "band"), P())
    return jax.shard_map(body, mesh=mesh, in_specs=in_specs, out_specs=out_specs, check_vma=False)
```

```python
import functools
import math

import jax
import jax.numpy as jnp
import ml_dtypes
import numpy as np
from jax import lax
from jax.experimental import pallas as pl
from jax.experimental.pallas import tpu as pltpu
from jax.sharding import PartitionSpec as P

NX = 144
NY = 144
NZ = 288
HALF = 64
LANES = 128
KINETIC = 8.0
HIGHEST = lax.Precision.HIGHEST
F32 = jnp.float32
BF16 = jnp.bfloat16
MESH = pl.DeviceIdType.MESH


def frequency(position, length):
    return jnp.where(position < (length + 1) // 2, position, position - length).astype(F32)


def angles(rows, columns, length):
    phase = np.outer(np.arange(rows), np.arange(columns)) % length
    return 2.0 * np.pi / length * phase


def split_table(table):
    high = table.astype(np.float32).astype(ml_dtypes.bfloat16)
    low = (table - high.astype(np.float64)).astype(np.float32).astype(ml_dtypes.bfloat16)
    return high, low


def plane_table(length):
    angle = angles(length, length, length)
    return split_table(np.concatenate([np.cos(angle), np.sin(angle)], 0))


def normal_tables(devices, planes, padded):
    angle = angles(NZ, NZ, NZ)
    cosine, sine = np.cos(angle), np.sin(angle)
    forward = np.zeros((devices, 2, padded, 2, NZ))
    forward[:, 0, :planes, 0] = cosine.reshape(devices, planes, NZ)
    forward[:, 0, :planes, 1] = -sine.reshape(devices, planes, NZ)
    forward[:, 1, :planes, 0] = sine.reshape(devices, planes, NZ)
    forward[:, 1, :planes, 1] = cosine.reshape(devices, planes, NZ)
    forward = forward.reshape(devices * 2 * padded, 2 * NZ)
    return split_table(forward), split_table(forward.T.copy())


def split_value(value):
    high = value.astype(BF16)
    low = (value - high.astype(F32)).astype(BF16)
    return high, low


def dot3(table_high, table_low, value):
    high, low = split_value(value)
    dot = functools.partial(jnp.dot, preferred_element_type=F32)
    return dot(table_high, high) + dot(table_low, high) + dot(table_high, low)


def fft_peer(i, count):
    return lax.axis_index("band"), lax.rem(lax.axis_index("fft") + i, count)


def band_peer(i, count):
    return lax.rem(lax.axis_index("band") + i, count), lax.axis_index("fft")


def greet(peer, count):
    barrier = pltpu.get_barrier_semaphore()
    for i in range(1, count):
        pl.semaphore_signal(barrier, inc=1, device_id=peer(i, count), device_id_type=MESH)


def exchange(peer, count, source, slots, send, receive):
    copies = []
    for i in range(1, count):
        copy = pltpu.make_async_remote_copy(
            src_ref=source(i),
            dst_ref=slots.at[i],
            send_sem=send.at[i],
            recv_sem=receive.at[i],
            device_id=peer(i, count),
            device_id_type=MESH,
        )
        copy.start()
        copies.append(copy)
    return copies


def swap_blocks(count, blocks, slots, send, receive):
    fft = lax.axis_index("fft")
    return exchange(
        fft_peer, count, lambda i: blocks.at[lax.rem(fft + i, count)], slots, send, receive
    )


def fold(row):
    return sum(row[:, i : i + LANES] for i in range(0, row.shape[1], LANES))


def normal_kernel(
    planes,
    orbital_ref,
    height_ref,
    high_ref,
    low_ref,
    projector_ref,
    landed_ref,
    out_ref,
    slots_in,
    send,
    receive,
    dense,
    slot_heights,
    slot_values,
    held,
    partial,
    arrived,
):
    slots, sticks = height_ref.shape
    projector_count = projector_ref.shape[1]
    fetch = pltpu.make_async_copy(projector_ref, held, arrived)
    fetch.start()
    greet(fft_peer, landed_ref.shape[0])
    block = NZ // 2
    base = lax.broadcasted_iota(jnp.int32, (block, LANES), 0)
    for lane in range(0, sticks, LANES):
        slot_heights[...] = height_ref[:, lane : lane + LANES]
        slot_values[0] = orbital_ref[0, 0, :, lane : lane + LANES]
        slot_values[1] = orbital_ref[1, 0, :, lane : lane + LANES]
        for start in range(0, NZ, block):

            def step(slot, carry):
                real, imag = carry
                here = base + start == slot_heights[pl.ds(slot, 1), :]
                row_r = slot_values[0, pl.ds(slot, 1), :]
                row_i = slot_values[1, pl.ds(slot, 1), :]
                return jnp.where(here, row_r, real), jnp.where(here, row_i, imag)

            zero = jnp.zeros((block, LANES), F32)
            real, imag = lax.fori_loop(0, slots, step, (zero, zero), unroll=4)
            dense[start : start + block, lane : lane + LANES] = real
            dense[NZ + start : NZ + start + block, lane : lane + LANES] = imag
    result = dot3(high_ref[...], low_ref[...], dense[...])
    devices = out_ref.shape[0]
    padded = result.shape[0] // (2 * devices)
    for device in range(devices):
        for part in range(2):
            first = (device * 2 + part) * padded
            out_ref[device, part * padded : (part + 1) * padded, :] = result[
                first : first + padded
            ]
    fetch.wait()
    partial[...] = jnp.zeros_like(partial)
    orb_r, orb_i = orbital_ref[0, 0], orbital_ref[1, 0]
    for k in range(projector_count):
        pr, pi = held[0, k], held[1, k]
        real = jnp.sum(pr * orb_r + pi * orb_i, axis=0, keepdims=True)
        imag = jnp.sum(pr * orb_i - pi * orb_r, axis=0, keepdims=True)
        partial[k : k + 1, :] = fold(real)
        partial[HALF + k : HALF + k + 1, :] = fold(imag)
    sums = jnp.sum(partial[...].T, axis=0, keepdims=True)
    sums = jnp.concatenate([sums] + [jnp.zeros_like(sums)] * (sticks // LANES - 1), 1)
    sums = jnp.broadcast_to(sums, (8, sticks))
    for device in range(devices):
        out_ref[device, 2 * padded :, :] = sums
    pl.semaphore_wait(pltpu.get_barrier_semaphore(), devices - 1)
    copies = swap_blocks(devices, out_ref, slots_in, send, receive)
    fft = lax.axis_index("fft")
    landed_ref[fft] = out_ref[fft]
    for i, copy in enumerate(copies, 1):
        copy.wait()
        landed_ref[lax.rem(fft - i + devices, devices)] = slots_in[i]


def plane_kernel(
    column_ref, received_ref, potential_ref, table_ref, out_ref, total_ref, grid, factor, wide, tall, rows
):
    devices, _, sticks = received_ref.shape
    planes = potential_ref.shape[0]
    padded = (received_ref.shape[1] - 8) // 2
    total = devices * sticks
    points = NX * NY
    lane = lax.broadcasted_iota(jnp.int32, (1, LANES), 1)
    sign = jnp.where(lane < HALF, -1.0, 1.0).astype(F32)

    tall[...] = jnp.zeros_like(tall)
    tall[0:planes, :] = potential_ref[...]

    def lay(index, carry):
        at = pl.ds(pl.multiple_of(index * LANES, LANES), LANES)
        piece = tall[:, at]
        factor[at, :] = jnp.concatenate([piece, piece], 0).T
        return carry

    lax.fori_loop(0, points // LANES, lay, 0, unroll=9)

    wide[...] = jnp.zeros_like(wide)
    for device in range(devices):
        for part in range(2):
            wide[part * HALF : part * HALF + padded, device * sticks : (device + 1) * sticks] = (
                received_ref[device, part * padded : (part + 1) * padded, :]
            )
    total_ref[...] = sum(received_ref[device, 2 * padded :, 0:LANES] for device in range(devices))
    for first in range(0, total, LANES):
        rows[first : first + LANES, :] = wide[:, first : first + LANES].T

    def clear(index, carry):
        grid[pl.ds(pl.multiple_of(index * NY, 8), NY), :] = jnp.zeros((NY, LANES), F32)
        return carry

    lax.fori_loop(0, NX, clear, 0, unroll=4)

    def put(stick, carry):
        grid[pl.ds(column_ref[stick], 1), :] = rows[pl.ds(stick, 1), :]
        return carry

    lax.fori_loop(0, total, put, 0, unroll=16)

    def transform(value, direction):
        high, low = split_value(value)
        product = jnp.dot(
            table_ref[...], jnp.concatenate([high, low, high], 0), preferred_element_type=F32
        )
        length = product.shape[0] // 2
        turned = [
            product[:length, i : i + LANES]
            + (direction * sign) * pltpu.roll(product[length:, i : i + LANES], HALF, 1)
            for i in range(0, 2 * LANES, LANES)
        ]
        return turned

    def along_y(direction):
        def step(pair, carry):
            first = pl.ds(pl.multiple_of(pair * 2 * NY, 8), NY)
            second = pl.ds(pl.multiple_of((pair * 2 + 1) * NY, 8), NY)
            left, right = transform(jnp.concatenate([grid[first, :], grid[second, :]], 1), direction)
            grid[first, :] = left
            grid[second, :] = right
            return carry

        lax.fori_loop(0, NX // 2, step, 0, unroll=6)

    def along_x(pair, carry):
        first = pl.ds(pair * 2, NX, stride=NY)
        second = pl.ds(pair * 2 + 1, NX, stride=NY)
        left, right = transform(jnp.concatenate([grid[first, :], grid[second, :]], 1), 1.0)
        left = left * factor[first, :]
        right = right * factor[second, :]
        left, right = transform(jnp.concatenate([left, right], 1), -1.0)
        grid[first, :] = left
        grid[second, :] = right
        return carry

    along_y(1.0)
    lax.fori_loop(0, NY // 2, along_x, 0, unroll=6)
    along_y(-1.0)

    def take(stick, carry):
        rows[pl.ds(stick, 1), :] = grid[pl.ds(column_ref[stick], 1), :]
        return carry

    lax.fori_loop(0, total, take, 0, unroll=8)
    for first in range(0, total, LANES):
        device, start = first // sticks, first % sticks
        piece = rows[first : first + LANES, :].T
        for part in range(2):
            out_ref[device, part * padded : (part + 1) * padded, start : start + LANES] = piece[
                part * HALF : part * HALF + padded
            ]


def final_kernel(
    weight_ref,
    value_ref,
    high_ref,
    low_ref,
    height_ref,
    plane_kinetic_ref,
    orbital_ref,
    projector_any,
    all_any,
    out_ref,
    column_ref,
    projector_ref,
    all_ref,
    fetched,
    slots_in,
    back_ref,
    send,
    receive,
    sum_ref,
    own,
    summed,
    fft_in,
    band_in,
    fft_send,
    fft_receive,
    band_send,
    band_receive,
    spectrum,
):
    devices, double, sticks = back_ref.shape
    band_count = column_ref.shape[0]
    first_fetch = pltpu.make_async_copy(projector_any, projector_ref, fetched.at[0])
    second_fetch = pltpu.make_async_copy(all_any, all_ref, fetched.at[1])
    first_fetch.start()
    second_fetch.start()
    greet(fft_peer, devices)
    greet(band_peer, band_count)
    pl.semaphore_wait(pltpu.get_barrier_semaphore(), devices + band_count - 2)
    copies = swap_blocks(devices, value_ref, slots_in, send, receive)
    fft, mine = lax.axis_index("fft"), lax.axis_index("band")
    back_ref[fft] = value_ref[fft]
    first_fetch.wait()
    second_fetch.wait()
    padded = double // 2
    slots = height_ref.shape[0]
    projector_count = projector_ref.shape[1]
    band_total = all_ref.shape[1]
    grid_total = NX * NY * NZ
    row_count = 48
    for first in range(0, slots, row_count):
        at = slice(first, first + row_count)
        for lane in range(0, sticks, LANES):
            lanes = slice(lane, lane + LANES)
            along_z = frequency(height_ref[at, lanes], NZ) / NZ
            kinetic = plane_kinetic_ref[:, lanes] + KINETIC * along_z * along_z
            real = jnp.zeros((row_count, LANES), F32)
            imag = jnp.zeros((row_count, LANES), F32)
            for k in range(projector_count):
                pr = projector_ref[0, k, at, lanes]
                pi = projector_ref[1, k, at, lanes]
                wr, wi = weight_ref[0, k], weight_ref[1, k]
                real = real + (pr * wr - pi * wi)
                imag = imag + (pr * wi + pi * wr)
            out_ref[0, 0, at, lanes] = (
                kinetic * orbital_ref[0, 0, at, lanes] + real
            )
            out_ref[1, 0, at, lanes] = (
                kinetic * orbital_ref[1, 0, at, lanes] + imag
            )
    for i, copy in enumerate(copies, 1):
        copy.wait()
        back_ref[lax.rem(fft - i + devices, devices)] = slots_in[i]
    back = back_ref[...].reshape(devices * 2 * padded, sticks)
    result = dot3(high_ref[...], low_ref[...], back)
    for lane in range(0, sticks, LANES):
        spectrum[lane // LANES] = result[:, lane : lane + LANES]
    for lane in range(0, sticks, LANES):
        lanes = slice(lane, lane + LANES)
        heights = height_ref[:, lanes]

        def step(height, carry):
            real, imag = carry
            here = heights == height
            row_r = spectrum[lane // LANES, pl.ds(height, 1), :]
            row_i = spectrum[lane // LANES, pl.ds(NZ + height, 1), :]
            return jnp.where(here, row_r, real), jnp.where(here, row_i, imag)

        zero = jnp.zeros((slots, LANES), F32)
        real, imag = lax.fori_loop(0, NZ, step, (zero, zero), unroll=4)
        out_ref[0, 0, :, lanes] = out_ref[0, 0, :, lanes] + real / grid_total
        out_ref[1, 0, :, lanes] = out_ref[1, 0, :, lanes] + imag / grid_total
    for band in range(band_total):
        hr, hi = out_ref[0, 0], out_ref[1, 0]
        br, bi = all_ref[0, band], all_ref[1, band]
        sum_ref[band : band + 1, :] = jnp.sum(br * hr + bi * hi, axis=0, keepdims=True)
        sum_ref[band_total + band : band_total + band + 1, :] = jnp.sum(br * hi - bi * hr, axis=0, keepdims=True)
    own[...] = fold(sum_ref[...])
    for copy in exchange(fft_peer, devices, lambda i: own, fft_in, fft_send, fft_receive):
        copy.wait()
    fft_in[0] = own[...]
    total = jnp.zeros_like(own)
    for i in range(devices):
        total = total + fft_in[lax.rem(fft - i + devices, devices)]
    summed[...] = total
    for copy in exchange(band_peer, band_count, lambda i: summed, band_in, band_send, band_receive):
        copy.wait()
    band_in[0] = summed[...]
    for i in range(band_count):
        column_ref[i] = band_in[lax.rem(mine - i + band_count, band_count)]


def params(mebibytes, number=None):
    return pltpu.CompilerParams(
        vmem_limit_bytes=mebibytes << 20, collective_id=number, has_side_effects=number is not None
    )


def body(orbitals, potential, projectors, coupling, stick_column, stick_heights, projector_atom):
    slot_count = orbitals.shape[2]
    sticks_here = orbitals.shape[3]
    projector_count = projectors.shape[1]
    planes_here = potential.shape[0]
    devices = NZ // planes_here
    stick_total = stick_column.shape[0]
    coeff_total = slot_count * stick_total
    padded = -(-planes_here // 8) * 8
    vmem = pl.BlockSpec(memory_space=pltpu.VMEM)
    smem = pl.BlockSpec(memory_space=pltpu.SMEM)
    (z_high, z_low), (back_high, back_low) = normal_tables(devices, planes_here, padded)
    plane_high, plane_low = plane_table(NX)
    plane_triple = np.concatenate([plane_high, plane_high, plane_low], 1)

    all_orbitals = lax.all_gather(orbitals, "band", axis=1, tiled=True)
    band_total = all_orbitals.shape[1]
    first_stick = lax.axis_index("fft") * sticks_here
    local_columns = lax.dynamic_slice_in_dim(stick_column, first_stick, sticks_here)
    along_x = frequency(local_columns // NY, NX) / NX
    along_y = frequency(local_columns % NY, NY) / NY
    plane_kinetic = (KINETIC * (along_x * along_x + along_y * along_y))[None, :]

    forth = (devices, 2 * padded + 8, sticks_here)
    back = (devices, 2 * padded, sticks_here)
    anywhere = pl.BlockSpec(memory_space=pl.ANY)
    received = pl.pallas_call(
        functools.partial(normal_kernel, planes_here),
        in_specs=[vmem] * 4 + [anywhere],
        out_specs=vmem,
        out_shape=jax.ShapeDtypeStruct(forth, F32),
        scratch_shapes=[
            pltpu.VMEM(forth, F32),
            pltpu.VMEM(forth, F32),
            pltpu.SemaphoreType.DMA((devices,)),
            pltpu.SemaphoreType.DMA((devices,)),
            pltpu.VMEM((2 * NZ, sticks_here), F32),
            pltpu.VMEM((slot_count, LANES), jnp.int32),
            pltpu.VMEM((2, slot_count, LANES), F32),
            pltpu.VMEM(projectors.shape, F32),
            pltpu.VMEM((LANES, LANES), F32),
            pltpu.SemaphoreType.DMA,
        ],
        compiler_params=params(56, 0),
        cost_estimate=pl.CostEstimate(flops=600000000, bytes_accessed=3000000, transcendentals=0),
    )(orbitals, stick_heights, z_high, z_low, projectors)
    values, total = pl.pallas_call(
        plane_kernel,
        in_specs=[smem] + [vmem] * 3,
        out_specs=(vmem, vmem),
        out_shape=(jax.ShapeDtypeStruct(back, F32), jax.ShapeDtypeStruct((8, LANES), F32)),
        scratch_shapes=[
            pltpu.VMEM((NX * NY, LANES), F32),
            pltpu.VMEM((NX * NY, LANES), F32),
            pltpu.VMEM((2 * HALF, stick_total), F32),
            pltpu.VMEM((HALF, NX * NY), F32),
            pltpu.VMEM((stick_total, LANES), F32),
        ],
        compiler_params=params(56),
        cost_estimate=pl.CostEstimate(
            flops=60000000000, bytes_accessed=6000000, transcendentals=0
        ),
    )(stick_column, received, potential, plane_triple)
    norm_scale = 1.0 / math.sqrt(coeff_total)
    total = total[0].reshape(2, HALF)[:, :projector_count, None]
    projections = total * norm_scale
    same_atom = projector_atom[:, None] == projector_atom[None, :]
    atom_coupling = jnp.where(same_atom, 0.5 * (coupling + coupling.T), jnp.zeros_like(coupling))
    weighted = jnp.einsum("kl,plb->pkb", atom_coupling, projections, precision=HIGHEST)
    band_devices = band_total // orbitals.shape[1]
    rows = 2 * band_total
    applied_h, gathered = pl.pallas_call(
        final_kernel,
        in_specs=[smem] + [vmem] * 6 + [anywhere] * 2,
        out_specs=(vmem, vmem),
        out_shape=(
            jax.ShapeDtypeStruct(orbitals.shape, F32),
            jax.ShapeDtypeStruct((band_devices, rows, LANES), F32),
        ),
        scratch_shapes=[
            pltpu.VMEM(projectors.shape, F32),
            pltpu.VMEM(all_orbitals.shape, F32),
            pltpu.SemaphoreType.DMA((2,)),
            pltpu.VMEM(back, F32),
            pltpu.VMEM(back, F32),
            pltpu.SemaphoreType.DMA((devices,)),
            pltpu.SemaphoreType.DMA((devices,)),
            pltpu.VMEM((rows, sticks_here), F32),
            pltpu.VMEM((rows, LANES), F32),
            pltpu.VMEM((rows, LANES), F32),
            pltpu.VMEM((devices, rows, LANES), F32),
            pltpu.VMEM((band_devices, rows, LANES), F32),
            pltpu.SemaphoreType.DMA((devices,)),
            pltpu.SemaphoreType.DMA((devices,)),
            pltpu.SemaphoreType.DMA((band_devices,)),
            pltpu.SemaphoreType.DMA((band_devices,)),
            pltpu.VMEM((sticks_here // LANES, 2 * NZ, LANES), F32),
        ],
        compiler_params=params(56, 1),
        cost_estimate=pl.CostEstimate(flops=600000000, bytes_accessed=9000000, transcendentals=0),
    )(
        weighted[:, :, 0] * norm_scale,
        values,
        back_high,
        back_low,
        stick_heights,
        plane_kinetic,
        orbitals,
        projectors,
        all_orbitals,
    )
    subspace = jnp.sum(gathered, axis=2).reshape(band_devices, 2, band_total)
    subspace = jnp.transpose(subspace, (1, 2, 0)) / coeff_total
    return (applied_h, projections, subspace)


def solution(mesh):
    in_specs = (
        P(None, "band", None, "fft"),
        P("fft", None),
        P(None, None, None, "fft"),
        P(),
        P(),
        P(None, "fft"),
        P(),
    )
    out_specs = (P(None, "band", None, "fft"), P(None, None, "band"), P())
    return jax.shard_map(body, mesh=mesh, in_specs=in_specs, out_specs=out_specs, check_vma=False)
```
